128 devices in a mesh: row: 16 (over x, y), col: 8 (over z, core).
Axes of the slice: x: 4, y: 4, z: 4, core: 2. Of those that a mesh axis runs over, the one named last changes fastest.
Arguments:
- tile_values: bfloat16 [128, 8, 4, 256, 256], P('row', 'col'), may hold values from 0 to 1, as said below
- tile_cols: int32 [128, 8, 4], P('row', 'col'), may hold values from 0 to 15, as said below
- row_counts: int32 [128, 8], P('row', 'col'), may hold values from 1 to 4, as said below
- start_basis: bfloat16 [64, 32768], P(None, ('row', 'col')), may hold values from -6 to 6
Outputs:
- embedding: float32 [64, 32768], P(None, ('row', 'col'))
- degrees: float32 [32768], P(('row', 'col'))
The draws below stay inside these ranges and needn't reach their ends.
Inputs may be any that keep to these rules, and one draw needn't show every extreme that they name: `tile_values`: entries are positive. `tile_cols`: within one tile row and column class the numbers of the 4 slots are distinct. Over the 8 tile rows that one device stores in its column class, no number occurs in more than 2 slots, live or empty, and one number, the same on every device of that column class, occurs in 2 live slots. `row_counts`: some entry equals 4.
All inputs are finite; a program needn't handle non-finite values.
Results may differ from the reference program's by a relative error of at most 0.009.
Values may be sent and summed in bfloat16 or wider, within the bound.
No kernel may reach another device: no remote copies, remote signals or barrier semaphores. Data moves between devices by JAX's collectives and lax.ppermute only.
A program may use at most 64 MiB of HBM per device.

```python
import math
import jax
import jax.numpy as jnp
from jax import lax

TILE = 256
COLS = 64
SLOTS = 4
STEPS = 3
PANELS = 128
MOST = 2
N_ROW = 16
N_COL = 8


def column_numbers(key):
    score_key = jax.random.fold_in(key, 31)
    block_key = jax.random.fold_in(key, 32)
    hot_block = jax.random.randint(block_key, (N_COL,), 0, N_ROW)
    scores = jax.random.randint(score_key, (N_ROW, N_COL, N_ROW), 0, 1 << 20) * N_ROW + jnp.arange(N_ROW, dtype=jnp.int32)
    scores = jnp.where(jnp.arange(N_ROW, dtype=jnp.int32) == 0, -1, scores)
    order = jnp.argsort(scores, axis=-1).astype(jnp.int32)
    shuffled = (hot_block[None, :, None] + order) % N_ROW
    cycle_length = N_COL * SLOTS // MOST
    position = (jnp.arange(N_COL)[:, None] * SLOTS + jnp.arange(SLOTS)[None, :]) % cycle_length
    picked = jnp.take(shuffled, position.reshape(-1), axis=2).reshape(N_ROW, N_COL, N_COL, SLOTS)
    return picked.transpose(0, 2, 1, 3).reshape(PANELS, N_COL, SLOTS).astype(jnp.int32)


def draw_tile_cols(key, part):
    return column_numbers(key)


def panel_levels(lowest):
    ramp = jnp.arange(PANELS, dtype=jnp.float32) / max(PANELS - 1, 1)
    return jnp.exp(math.log(lowest) * (1.0 - ramp))


def draw_tile_values(key, part):
    columns = column_numbers(key)
    groups = max(TILE // 4, 2)
    coupling = 0.3 / groups
    labels = jax.random.randint(jax.random.fold_in(key, 41), (PANELS, TILE), 0, groups)
    activity = jnp.exp(jax.random.uniform(jax.random.fold_in(key, 44), (PANELS, TILE), jnp.float32, math.log(0.001), 0.0))
    col_panel = columns * N_COL + jnp.arange(N_COL, dtype=jnp.int32)[None, :, None]
    row_labels = labels[:, None, None, :, None]
    col_labels = labels[col_panel][:, :, :, None, :]
    joined = row_labels == col_labels
    row_activity = activity[:, None, None, :, None]
    col_activity = activity[col_panel][:, :, :, None, :]
    full_shape = (PANELS, N_COL, SLOTS, TILE, TILE)
    weight = jnp.exp(jax.random.uniform(jax.random.fold_in(key, 43), full_shape, jnp.float32, math.log(0.05), 0.0))
    levels = panel_levels(0.1)
    tile_scale = jnp.sqrt(levels[:, None, None] * levels[col_panel])
    values = weight * tile_scale[:, :, :, None, None] * jnp.where(joined, 1.0, coupling) * row_activity * col_activity
    return values.astype(jnp.bfloat16)


def draw_row_counts(key, part):
    heat_key = jax.random.fold_in(key, 11)
    cell_key = jax.random.fold_in(key, 12)
    pick_key = jax.random.fold_in(key, 13)
    heat = jax.random.randint(heat_key, (PANELS, 1), 1, SLOTS + 1)
    counts = jax.random.randint(cell_key, (PANELS, N_COL), 0, 1 << 20) % heat + 1
    chosen = jax.random.randint(pick_key, (), 0, PANELS * N_COL)
    flat_index = jnp.arange(PANELS * N_COL, dtype=jnp.int32).reshape(PANELS, N_COL)
    return jnp.where(flat_index == chosen, SLOTS, counts).astype(jnp.int32)


def draw_start_basis(key, part):
    key = jax.random.fold_in(key, 5)
    offset_key = jax.random.fold_in(key, 1)
    noise_key = jax.random.fold_in(key, 2)
    ramp = 0.25 + 1.5 * jnp.arange(PANELS, dtype=jnp.float32) / max(PANELS - 1, 1)
    spread = jnp.repeat(ramp, TILE)
    offsets = jax.random.uniform(offset_key, (COLS, 1), jnp.float32, -1.0, 1.0)
    noise = jnp.clip(jax.random.normal(noise_key, (COLS, PANELS * TILE), jnp.float32), -4.0, 4.0)
    return (offsets * spread[None, :] + noise).astype(jnp.bfloat16)


def setup_inputs(seed: int = 0) -> dict:
    key_list = jax.random.split(jax.random.key(seed), 5)
    return {
        "tile_values": draw_tile_values(jax.random.fold_in(key_list[4], 71), 0),
        "tile_cols": draw_tile_cols(jax.random.fold_in(key_list[4], 71), 0),
        "row_counts": draw_row_counts(jax.random.fold_in(key_list[4], 71), 0),
        "start_basis": draw_start_basis(jax.random.fold_in(key_list[4], 71), 0),
    }


EPSILON = 1e-06
RESTART = 0.2

def reference(tile_values, tile_cols, row_counts, start_basis):
    panels = N_ROW * N_COL
    total_cells = panels * TILE
    live_mask = (jnp.arange(SLOTS)[None, None, :] < row_counts[:, :, None]).astype(jnp.float32)
    col_panel = (tile_cols * N_COL + jnp.arange(N_COL, dtype=jnp.int32)[None, :, None]).astype(jnp.int32)

    def tile_sums(pair):
        tiles, mask = pair
        wide = tiles.astype(jnp.float32)
        row_total = jnp.einsum('csuv,cs->u', wide, mask)
        col_total = jnp.einsum('csuv,cs->csv', wide, mask)
        return (row_total, col_total)
    row_part, col_local = lax.map(tile_sums, (tile_values, live_mask))
    col_part = jax.ops.segment_sum(col_local.reshape(-1, TILE), col_panel.reshape(-1), num_segments=panels)
    degrees = (row_part + col_part).reshape(total_cells)

    def apply_operator(weighted):
        blocks = weighted.astype(jnp.float32).reshape(COLS, panels, TILE).transpose(1, 0, 2)

        def visit(carry, item):
            tiles, mask, target, own_block = item
            wide = tiles.astype(jnp.float32)
            picked = blocks[target] * mask[:, :, None, None]
            forward = jnp.einsum('cskv,csuv->ku', picked, wide)
            reverse = jnp.einsum('ku,csuv->cskv', own_block, wide) * mask[:, :, None, None]
            carry = carry.at[target.reshape(-1)].add(reverse.reshape(-1, COLS, TILE))
            return (carry, forward)
        initial = jnp.zeros((panels, COLS, TILE), jnp.float32)
        back_total, forward_all = lax.scan(visit, initial, (tile_values, live_mask, col_panel, blocks))
        return (forward_all + back_total).transpose(1, 0, 2).reshape(COLS, total_cells)
    volume = jnp.sum(degrees)
    inv_root = 1.0 / jnp.sqrt(degrees + volume / total_cells)
    leading = jnp.sqrt(degrees / volume)
    start_wide = start_basis.astype(jnp.float32)
    current = start_basis
    for repeat in range(STEPS):
        weighted = (inv_root[None, :] * current.astype(jnp.float32)).astype(jnp.bfloat16)
        applied = inv_root[None, :] * apply_operator(weighted)
        projection = lax.optimization_barrier(jnp.sum(current.astype(jnp.float32) * leading[None, :], axis=1))
        residual = applied - projection[:, None] * leading[None, :]
        norms = lax.optimization_barrier(jnp.sum(residual * residual, axis=1))
        scaled = residual / jnp.sqrt(norms / total_cells + EPSILON)[:, None]
        blend = (1.0 - RESTART) * scaled + RESTART * start_wide
        current = blend.astype(jnp.bfloat16) if repeat + 1 < STEPS else blend
    return (current, degrees)
```

```python
import jax
import jax.numpy as jnp
from jax import lax
from jax.experimental import pallas as pl
from jax.experimental.pallas import tpu as pltpu
from jax.sharding import PartitionSpec as P

STEPS = 3
EPSILON = 1e-06
RESTART = 0.2

F32 = jnp.float32
BF16 = jnp.bfloat16
VMEM = pl.BlockSpec(memory_space=pltpu.VMEM)
SMEM = pl.BlockSpec(memory_space=pltpu.SMEM)
PARAMS = pltpu.CompilerParams(vmem_limit_bytes=40 * 1024 * 1024)
EXTRA = 16


def nn(a, b):
    return lax.dot_general(a, b, (((1,), (0,)), ((), ())), preferred_element_type=F32)


def nt(a, b):
    return lax.dot_general(a, b, (((1,), (1,)), ((), ())), preferred_element_type=F32)


def call(kernel, outs, ins, out_specs=None, scratch=(), flops=1e6, moved=1e6):
    return pl.pallas_call(
        kernel,
        out_shape=outs,
        in_specs=ins,
        out_specs=out_specs if out_specs is not None else jax.tree.map(lambda _: VMEM, outs),
        scratch_shapes=list(scratch),
        compiler_params=PARAMS,
        cost_estimate=pl.CostEstimate(
            flops=int(flops), bytes_accessed=int(moved), transcendentals=0
        ),
    )


def to_rows(first, second):
    cells = first.shape[0]
    lane = lax.broadcasted_iota(jnp.int32, (cells, 128), 1)
    wide = jnp.where(lane == 0, first, jnp.where(lane == 1, second, 0.0))
    wide = jnp.concatenate([wide, jnp.zeros((128 - cells, 128), F32)], axis=0)
    return wide.T[:8]


def to_columns(block, cells):
    wide = jnp.concatenate([block, jnp.zeros((120, 128), F32)], axis=0).T
    return wide[:cells, 0:1], wide[:cells, 1:2]


def degree_kernel(place, columns, counts, tiles, message, table, row_sums, col_sums, used):
    panels, slots, tile = tiles.shape[0], tiles.shape[1], tiles.shape[2]
    row_devices = message.shape[0]
    mine_row, mine_col = place[0], place[1]

    for b in range(row_devices):
        used[b] = 0
    for q in range(panels * slots):
        b = columns[q]
        table[2 * b + used[b]] = q
        used[b] = used[b] + 1

    ones = jnp.ones((16, tile), BF16)
    for i in range(panels):
        total = jnp.zeros((16, tile), F32)
        for s in range(slots):
            live = s < counts[i]
            weight = jnp.where(live, ones, jnp.zeros_like(ones))
            value = tiles[i, s]
            total = total + nt(weight, value)
            col_sums[i * slots + s] = nn(weight, value)[:8]
        row_sums[i : i + 1, :] = total[:1]
    rows = row_sums[...]
    everything = jnp.sum(jnp.sum(rows, axis=1, keepdims=True), axis=0, keepdims=True)
    for b in range(row_devices):
        part = col_sums[table[2 * b]] + col_sums[table[2 * b + 1]]
        at = lax.broadcasted_iota(jnp.int32, part.shape, 0)
        part = jnp.where(at == mine_col, part, 0.0) + jnp.where(b == mine_row, rows, 0.0)
        message[b, :, :tile] = part
        message[b, :, tile:] = jnp.broadcast_to(everything, (part.shape[0], 128))


def pack(values, dots, many, one):
    cells = values.shape[0]
    body = values.astype(BF16)
    high = dots.astype(BF16)
    low = (dots - high.astype(F32)).astype(BF16)
    tail = jnp.concatenate([high, low], axis=0)
    tail = jnp.concatenate([tail, jnp.zeros_like(tail)], axis=1)
    one[...] = body
    for b in range(many.shape[0]):
        many[b, :cells] = body
        many[b, cells:] = tail


def start_kernel(total_cells, parts, start, degrees, scales, many, one):
    tile = start.shape[1]
    sums = jnp.sum(parts[...], axis=0, keepdims=True)
    degree = sums[:, :tile]
    volume = 2.0 * sums[:, tile : tile + 1]
    inv_root = 1.0 / jnp.sqrt(degree + volume / total_cells)
    leading = jnp.sqrt(degree / volume)
    degrees[...] = degree
    scales[0:1, :] = inv_root
    scales[1:2, :] = leading
    wide = start[...].astype(F32)
    dot = jnp.sum(wide * leading, axis=1, keepdims=True)
    pack(wide * inv_root, to_rows(dot, jnp.zeros_like(dot)), many, one)


def backward_kernel(place, table, counts, tiles, own, pair, far1, far3, far2, out):
    slots = tiles.shape[1]
    zs = tiles.shape[0] // 2
    mine_col = place[1]
    z, core = mine_col // 2, mine_col % 2
    panels = tiles.shape[0]
    buffer = out[1]
    result = out[0]
    for k, source in ((0, None), (1, far1), (2, far2), (3, far3)):
        at = (z + zs - k) % zs
        same = own[...] if source is None else source[0]
        other = pair[...] if source is None else source[1]
        buffer[2 * at + core] = same
        buffer[2 * at + 1 - core] = other
    for b in range(result.shape[0]):
        total = None
        for m in range(2):
            q = table[2 * b + m]
            i = q // slots
            s = q % slots
            panel = buffer[i]
            panel = jnp.where(s < counts[i], panel, jnp.zeros_like(panel))
            part = nn(panel, tiles[i, s])
            total = part if total is None else total + part
        result[b] = total


def forward_kernel(place, columns, counts, tiles, gathered, keep, give):
    panels, slots = tiles.shape[0], tiles.shape[1]
    cells = gathered.shape[1] - EXTRA
    zs = panels // 2
    z, core = place[1] // 2, place[1] % 2
    dots = jnp.zeros((8, 128), F32)
    for b in range(gathered.shape[0]):
        tail = gathered[b, cells:, :128].astype(F32)
        dots = dots + tail[:8] + tail[8:]
    dots = jnp.concatenate([dots, jnp.zeros_like(dots)], axis=1)
    for k in range(zs):
        at = (z + k) % zs
        for target, i in ((keep, 2 * at + core), (give, 2 * at + 1 - core)):
            total = None
            for s in range(slots):
                panel = gathered[columns[i * slots + s], :cells]
                panel = jnp.where(s < counts[i], panel, jnp.zeros_like(panel))
                part = nt(panel, tiles[i, s])
                total = part if total is None else total + part
            target[k, :cells] = total
            target[k, cells:] = dots


def gather_sums(tile_sums, near, far1, far3, far2, scales, cells):
    total = tile_sums[0]
    for b in range(1, tile_sums.shape[0]):
        total = total + tile_sums[b]
    side = near[...] + far1[...] + far2[...] + far3[...]
    product = (total + side[:cells]) * scales[0:1, :]
    return product, side[cells:, :128]


def first_kernel(tile_sums, near, far1, far3, far2, scales, many, one, applied, dots0, residual):
    cells = applied.shape[0]
    product, side = gather_sums(tile_sums, near, far1, far3, far2, scales, cells)
    projection, _ = to_columns(side, cells)
    applied[...] = product
    dots0[...] = side
    finish(product, projection, scales, many, one, residual)


def finish(applied, projection, scales, many, one, residual):
    inv_root, leading = scales[0:1, :], scales[1:2, :]
    rest = applied - projection * leading
    residual[...] = rest
    norm = jnp.sum(rest * rest, axis=1, keepdims=True)
    dot = jnp.sum(rest * leading, axis=1, keepdims=True)
    pack(rest * inv_root, to_rows(norm, dot), many, one)


def next_applied(total_cells, product, side, applied0, dots0, cells):
    norm, dot = to_columns(side, cells)
    start_dot, _ = to_columns(dots0[...], cells)
    scale = (1.0 - RESTART) / jnp.sqrt(norm / total_cells + EPSILON)
    applied = scale * product + RESTART * applied0[...]
    return applied, scale * dot + RESTART * start_dot


def middle_kernel(
    total_cells, tile_sums, near, far1, far3, far2, scales, applied0, dots0, many, one, residual
):
    cells = applied0.shape[0]
    product, side = gather_sums(tile_sums, near, far1, far3, far2, scales, cells)
    applied, projection = next_applied(total_cells, product, side, applied0, dots0, cells)
    finish(applied, projection, scales, many, one, residual)


def last_kernel(
    total_cells, tile_sums, near, far1, far3, far2, scales, applied0, dots0, norms, residual
):
    cells = applied0.shape[0]
    product, side = gather_sums(tile_sums, near, far1, far3, far2, scales, cells)
    applied, projection = next_applied(total_cells, product, side, applied0, dots0, cells)
    rest = applied - projection * scales[1:2, :]
    residual[...] = rest
    norm = jnp.sum(rest * rest, axis=1, keepdims=True)
    norms[...] = jnp.broadcast_to(to_rows(norm, norm)[:1], norms.shape)


def blend_kernel(total_cells, norms, residual, start, embedding):
    cells = start.shape[0]
    row = jnp.sum(norms[...], axis=0, keepdims=True)
    norm, _ = to_columns(jnp.concatenate([row, jnp.zeros((7, 128), F32)], axis=0), cells)
    scaled = residual[...] / jnp.sqrt(norm / total_cells + EPSILON)
    embedding[...] = (1.0 - RESTART) * scaled + RESTART * start[...].astype(F32)


def local(tile_values, tile_cols, row_counts, start_basis):
    rows, cols = lax.axis_size("row"), lax.axis_size("col")
    panels, _, slots, tile, _ = tile_values.shape
    cells = start_basis.shape[0]
    zs = cols // 2
    total_cells = rows * cols * tile
    tiles = tile_values.reshape(panels, slots, tile, tile)
    columns = tile_cols.reshape(panels * slots)
    counts = row_counts.reshape(panels)
    place = jnp.stack([lax.axis_index("row"), lax.axis_index("col")]).astype(jnp.int32)
    shape = jax.ShapeDtypeStruct
    swap = [(i, i ^ 1) for i in range(cols)]
    shift = lambda k: [(i, (i + 2 * k) % cols) for i in range(cols)]
    tile_bytes = panels * slots * tile * tile * 2
    work = 2 * panels * slots * cells * tile * tile

    message, table = call(
        degree_kernel,
        (shape((rows, cols, tile + 128), F32), shape((2 * rows,), jnp.int32)),
        [SMEM, SMEM, SMEM, VMEM],
        (VMEM, SMEM),
        [
            pltpu.VMEM((panels, tile), F32),
            pltpu.VMEM((panels * slots, 8, tile), F32),
            pltpu.SMEM((rows,), jnp.int32),
        ],
        work / 4,
        tile_bytes,
    )(place, columns, counts, tiles)
    parts = lax.all_to_all(
        message.reshape(rows * cols, tile + 128), ("row", "col"), 0, 0, tiled=True
    )

    many_shape = shape((rows, cells + EXTRA, tile), BF16)
    one_shape = shape((cells, tile), BF16)
    full = shape((cells, tile), F32)
    degrees, scales, many, one = call(
        lambda *refs: start_kernel(total_cells, *refs),
        (shape((1, tile), F32), shape((8, tile), F32), many_shape, one_shape),
        [VMEM, VMEM],
    )(parts, start_basis)

    applied0 = dots0 = residual = None
    for step in range(STEPS):
        pair = lax.ppermute(one, "col", swap)
        both = jnp.stack([one, pair])
        near = [lax.ppermute(both, "col", shift(k)) for k in (1, 3, 2)]
        gathered = lax.all_to_all(many, "row", 0, 0, tiled=True)
        back = call(
            lambda *refs: backward_kernel(*refs[:9], refs[9:]),
            shape((rows, cells, tile), F32),
            [SMEM, SMEM, SMEM] + [VMEM] * 6,
            VMEM,
            [pltpu.VMEM((panels, cells, tile), BF16)],
            work,
            tile_bytes,
        )(place, table, counts, tiles, one, pair, *near)
        back = lax.all_to_all(back, "row", 0, 0, tiled=True)
        side_shape = shape((zs, cells + 8, tile), F32)
        keep, give = call(
            forward_kernel,
            (side_shape, side_shape),
            [SMEM, SMEM, SMEM, VMEM, VMEM],
            flops=work,
            moved=tile_bytes,
        )(place, columns, counts, tiles, gathered)
        given = lax.ppermute(give, "col", swap)
        sums = keep + given
        sides = [sums[0]] + [lax.ppermute(sums[k], "col", shift(k)) for k in (1, 3, 2)]
        arrived = (back, *sides, scales)
        if step == 0:
            many, one, applied0, dots0, residual = call(
                first_kernel,
                (many_shape, one_shape, full, shape((8, 128), F32), full),
                [VMEM] * 6,
            )(*arrived)
        elif step + 1 < STEPS:
            many, one, residual = call(
                lambda *refs: middle_kernel(total_cells, *refs),
                (many_shape, one_shape, full),
                [VMEM] * 8,
            )(*arrived, applied0, dots0)
        else:
            norms, residual = call(
                lambda *refs: last_kernel(total_cells, *refs),
                (shape((rows * cols, 128), F32), full),
                [VMEM] * 8,
            )(*arrived, applied0, dots0)
    norms = lax.all_to_all(norms, ("row", "col"), 0, 0, tiled=True)
    embedding = call(
        lambda *refs: blend_kernel(total_cells, *refs), full, [VMEM] * 3
    )(norms, residual, start_basis)
    return (embedding, degrees.reshape(tile))


def solution(mesh):
    placed = (
        P("row", "col", None, None, None),
        P("row", "col", None),
        P("row", "col"),
        P(None, ("row", "col")),
    )
    return jax.shard_map(
        local,
        mesh=mesh,
        in_specs=placed,
        out_specs=(P(None, ("row", "col")), P(("row", "col"))),
        check_vma=False,
    )
```

```python
import jax
import jax.numpy as jnp
from jax import lax
from jax.experimental import pallas as pl
from jax.experimental.pallas import tpu as pltpu
from jax.sharding import PartitionSpec as P

STEPS = 3
EPSILON = 1e-06
RESTART = 0.2

F32 = jnp.float32
BF16 = jnp.bfloat16
VMEM = pl.BlockSpec(memory_space=pltpu.VMEM)
SMEM = pl.BlockSpec(memory_space=pltpu.SMEM)
EMPTY = 1024
COLUMNS = 8
SLOTS_OF = 64
META = 128
BACK = BF16
EXTRA = 16


def nn(a, b):
    return lax.dot_general(a, b, (((1,), (0,)), ((), ())), preferred_element_type=F32)


def nt(a, b):
    return lax.dot_general(a, b, (((1,), (1,)), ((), ())), preferred_element_type=F32)


def call(kernel, outs, ins, out_specs=None, scratch=(), flops=1e6, moved=1e6, limit=16 * 1024 * 1024):
    return pl.pallas_call(
        kernel,
        out_shape=outs,
        in_specs=ins,
        out_specs=out_specs if out_specs is not None else jax.tree.map(lambda _: VMEM, outs),
        scratch_shapes=list(scratch),
        compiler_params=pltpu.CompilerParams(vmem_limit_bytes=limit),
        cost_estimate=pl.CostEstimate(
            flops=int(flops), bytes_accessed=int(moved), transcendentals=0
        ),
    )


def to_rows(first, second):
    cells = first.shape[0]
    lane = lax.broadcasted_iota(jnp.int32, (cells, 128), 1)
    wide = jnp.where(lane == 0, first, jnp.where(lane == 1, second, 0.0))
    wide = jnp.concatenate([wide, jnp.zeros((128 - cells, 128), F32)], axis=0)
    return wide.T[:8]


def to_columns(block, cells):
    wide = jnp.concatenate([block, jnp.zeros((120, 128), F32)], axis=0).T
    return wide[:cells, 0:1], wide[:cells, 1:2]


def degree_kernel(place, columns, counts, tiles, message, meta, row_sums, col_sums, used):
    panels, slots, tile = tiles.shape[0], tiles.shape[1], tiles.shape[2]
    row_devices = message.shape[0]
    mine_row, mine_col = place[0], place[1]
    meta[0] = mine_row
    meta[1] = mine_col
    for b in range(row_devices):
        used[b] = 0
    for i in range(panels):
        for s in range(slots):
            q = i * slots + s
            b = columns[i, 0, s]
            dead = jnp.where(s < counts[i, 0], 0, EMPTY)
            meta[COLUMNS + q] = b + dead
            meta[SLOTS_OF + 2 * b + used[b]] = q + dead
            used[b] = used[b] + 1

    ones = jnp.ones((16, tile), BF16)
    for i in range(panels):
        total = jnp.zeros((16, tile), F32)
        for s in range(slots):
            live = s < counts[i, 0]
            weight = jnp.where(live, ones, jnp.zeros_like(ones))
            value = tiles[i, s]
            total = total + nt(weight, value)
            col_sums[i * slots + s] = nn(weight, value)[:8]
        row_sums[i : i + 1, :] = total[:1]
    rows = row_sums[...]
    everything = jnp.sum(jnp.sum(rows, axis=1, keepdims=True), axis=0, keepdims=True)
    for b in range(row_devices):
        first = meta[SLOTS_OF + 2 * b] % EMPTY
        second = meta[SLOTS_OF + 2 * b + 1] % EMPTY
        part = col_sums[first] + col_sums[second]
        at = lax.broadcasted_iota(jnp.int32, part.shape, 0)
        part = jnp.where(at == mine_col, part, 0.0) + jnp.where(b == mine_row, rows, 0.0)
        message[b, :, :tile] = part
        message[b, :, tile:] = jnp.broadcast_to(everything, (part.shape[0], 128))


def pack(values, dots, many, one):
    cells = values.shape[0]
    body = values.astype(BF16)
    high = dots.astype(BF16)
    low = (dots - high.astype(F32)).astype(BF16)
    tail = jnp.concatenate([high, low], axis=0)
    tail = jnp.concatenate([tail, jnp.zeros_like(tail)], axis=1)
    one[...] = body
    for b in range(many.shape[0]):
        many[b, :cells] = body
        many[b, cells:] = tail


def start_kernel(total_cells, parts, start, degrees, scales, many, one):
    tile = start.shape[1]
    sums = jnp.sum(parts[...], axis=0, keepdims=True)
    degree = sums[:, :tile]
    volume = 2.0 * sums[:, tile : tile + 1]
    inv_root = 1.0 / jnp.sqrt(degree + volume / total_cells)
    leading = jnp.sqrt(degree / volume)
    degrees[...] = degree
    scales[0:1, :] = inv_root
    scales[1:2, :] = leading
    wide = start[...].astype(F32)
    dot = jnp.sum(wide * leading, axis=1, keepdims=True)
    pack(wide * inv_root, to_rows(dot, jnp.zeros_like(dot)), many, one)


def product_kernel(
    meta, tiles, gathered, own, pair, far1, far3, far2, result, keep, give, buffer
):
    panels, slots = tiles.shape[0], tiles.shape[1]
    cells = own.shape[0]
    zs = panels // 2
    z, core = meta[1] // 2, meta[1] % 2
    dots = jnp.zeros((8, 128), F32)
    for b in range(gathered.shape[0]):
        tail = gathered[b, cells:, :128].astype(F32)
        dots = dots + tail[:8] + tail[8:]
    dots = jnp.concatenate([dots, jnp.zeros_like(dots)], axis=1)
    for k in range(zs):
        at = (z + k) % zs
        for target, i in ((keep, 2 * at + core), (give, 2 * at + 1 - core)):
            total = None
            for s in range(slots):
                held = meta[COLUMNS + i * slots + s]
                panel = gathered[held % EMPTY, :cells]
                panel = jnp.where(held < EMPTY, panel, jnp.zeros_like(panel))
                part = nt(panel, tiles[i, s])
                total = part if total is None else total + part
            target[k, :cells] = total
            target[k, cells:] = dots
    for k, source in ((0, None), (1, far1), (2, far2), (3, far3)):
        at = (z + zs - k) % zs
        same = own[...] if source is None else source[0]
        other = pair[...] if source is None else source[1]
        buffer[2 * at + core] = same
        buffer[2 * at + 1 - core] = other
    for b in range(result.shape[0]):
        total = None
        for m in range(2):
            held = meta[SLOTS_OF + 2 * b + m]
            q = held % EMPTY
            panel = buffer[q // slots]
            panel = jnp.where(held < EMPTY, panel, jnp.zeros_like(panel))
            part = nn(panel, tiles[q // slots, q % slots])
            total = part if total is None else total + part
        result[b] = total.astype(result.dtype)


def gather_sums(tile_sums, near, far1, far3, far2, scales, cells):
    total = tile_sums[0].astype(F32)
    for b in range(1, tile_sums.shape[0]):
        total = total + tile_sums[b].astype(F32)
    side = near[...] + far1[...] + far2[...] + far3[...]
    product = (total + side[:cells]) * scales[0:1, :]
    return product, side[cells:, :128]


def first_kernel(tile_sums, near, far1, far3, far2, scales, many, one, applied, dots0, residual):
    cells = applied.shape[0]
    product, side = gather_sums(tile_sums, near, far1, far3, far2, scales, cells)
    projection, _ = to_columns(side, cells)
    applied[...] = product
    dots0[...] = side
    finish(product, projection, scales, many, one, residual)


def finish(applied, projection, scales, many, one, residual):
    inv_root, leading = scales[0:1, :], scales[1:2, :]
    rest = applied - projection * leading
    residual[...] = rest
    norm = jnp.sum(rest * rest, axis=1, keepdims=True)
    dot = jnp.sum(rest * leading, axis=1, keepdims=True)
    pack(rest * inv_root, to_rows(norm, dot), many, one)


def next_applied(total_cells, product, side, applied0, dots0, cells):
    norm, dot = to_columns(side, cells)
    start_dot, _ = to_columns(dots0[...], cells)
    scale = (1.0 - RESTART) / jnp.sqrt(norm / total_cells + EPSILON)
    applied = scale * product + RESTART * applied0[...]
    return applied, scale * dot + RESTART * start_dot


def middle_kernel(
    total_cells, tile_sums, near, far1, far3, far2, scales, applied0, dots0, many, one, residual
):
    cells = applied0.shape[0]
    product, side = gather_sums(tile_sums, near, far1, far3, far2, scales, cells)
    applied, projection = next_applied(total_cells, product, side, applied0, dots0, cells)
    finish(applied, projection, scales, many, one, residual)


def last_kernel(
    total_cells, tile_sums, near, far1, far3, far2, scales, applied0, dots0, norms, residual
):
    cells = applied0.shape[0]
    product, side = gather_sums(tile_sums, near, far1, far3, far2, scales, cells)
    applied, projection = next_applied(total_cells, product, side, applied0, dots0, cells)
    rest = applied - projection * scales[1:2, :]
    residual[...] = rest
    norm = jnp.sum(rest * rest, axis=1, keepdims=True)
    norms[...] = jnp.broadcast_to(to_rows(norm, norm)[:1], norms.shape)


def blend_kernel(total_cells, norms, residual, start, embedding):
    cells = start.shape[0]
    row = jnp.sum(norms[...], axis=0, keepdims=True)
    norm, _ = to_columns(jnp.concatenate([row, jnp.zeros((7, 128), F32)], axis=0), cells)
    scaled = residual[...] / jnp.sqrt(norm / total_cells + EPSILON)
    embedding[...] = (1.0 - RESTART) * scaled + RESTART * start[...].astype(F32)


def local(tile_values, tile_cols, row_counts, start_basis):
    rows, cols = lax.axis_size("row"), lax.axis_size("col")
    panels, _, slots, tile, _ = tile_values.shape
    cells = start_basis.shape[0]
    zs = cols // 2
    total_cells = rows * cols * tile
    tiles = tile_values.reshape(panels, slots, tile, tile)
    place = jnp.stack([lax.axis_index("row"), lax.axis_index("col")]).astype(jnp.int32)
    shape = jax.ShapeDtypeStruct
    swap = [(i, i ^ 1) for i in range(cols)]
    shift = lambda k: [(i, (i + 2 * k) % cols) for i in range(cols)]
    tile_bytes = panels * slots * tile * tile * 2
    work = 2 * panels * slots * cells * tile * tile

    message, meta = call(
        degree_kernel,
        (shape((rows, cols, tile + 128), F32), shape((META,), jnp.int32)),
        [SMEM, SMEM, SMEM, VMEM],
        (VMEM, SMEM),
        [
            pltpu.VMEM((panels, tile), F32),
            pltpu.VMEM((panels * slots, 8, tile), F32),
            pltpu.SMEM((rows,), jnp.int32),
        ],
        work / 4,
        tile_bytes,
    )(place, tile_cols, row_counts, tiles)
    parts = lax.all_to_all(
        message.reshape(rows * cols, tile + 128), ("row", "col"), 0, 0, tiled=True
    )

    many_shape = shape((rows, cells + EXTRA, tile), BF16)
    one_shape = shape((cells, tile), BF16)
    full = shape((cells, tile), F32)
    degrees, scales, many, one = call(
        lambda *refs: start_kernel(total_cells, *refs),
        (shape((1, tile), F32), shape((8, tile), F32), many_shape, one_shape),
        [VMEM, VMEM],
    )(parts, start_basis)

    applied0 = dots0 = residual = None
    for step in range(STEPS):
        pair = lax.ppermute(one, "col", swap)
        both = jnp.stack([one, pair])
        near = [lax.ppermute(both, "col", shift(k)) for k in (1, 3, 2)]
        gathered = lax.all_to_all(many, "row", 0, 0, tiled=True)
        side_shape = shape((zs, cells + 8, tile), F32)
        back, keep, give = call(
            product_kernel,
            (shape((rows, cells, tile), BACK), side_shape, side_shape),
            [SMEM] + [VMEM] * 7,
            scratch=[pltpu.VMEM((panels, cells, tile), BF16)],
            flops=2 * work,
            moved=tile_bytes,
        )(meta, tiles, gathered, one, pair, *near)
        back = lax.all_to_all(back, "row", 0, 0, tiled=True)
        given = lax.ppermute(give, "col", swap)
        sums = keep + given
        sides = [sums[0]] + [lax.ppermute(sums[k], "col", shift(k)) for k in (1, 3, 2)]
        arrived = (back, *sides, scales)
        if step == 0:
            many, one, applied0, dots0, residual = call(
                first_kernel,
                (many_shape, one_shape, full, shape((8, 128), F32), full),
                [VMEM] * 6,
            )(*arrived)
        elif step + 1 < STEPS:
            many, one, residual = call(
                lambda *refs: middle_kernel(total_cells, *refs),
                (many_shape, one_shape, full),
                [VMEM] * 8,
            )(*arrived, applied0, dots0)
        else:
            norms, residual = call(
                lambda *refs: last_kernel(total_cells, *refs),
                (shape((rows * cols, 128), F32), full),
                [VMEM] * 8,
            )(*arrived, applied0, dots0)
    norms = lax.all_to_all(norms, ("row", "col"), 0, 0, tiled=True)
    embedding = call(
        lambda *refs: blend_kernel(total_cells, *refs), full, [VMEM] * 3
    )(norms, residual, start_basis)
    return (embedding, degrees.reshape(tile))


def solution(mesh):
    placed = (
        P("row", "col", None, None, None),
        P("row", "col", None),
        P("row", "col"),
        P(None, ("row", "col")),
    )
    return jax.shard_map(
        local,
        mesh=mesh,
        in_specs=placed,
        out_specs=(P(None, ("row", "col")), P(("row", "col"))),
        check_vma=False,
    )
```

```python
import jax
import jax.numpy as jnp
from jax import lax
from jax.experimental import pallas as pl
from jax.experimental.pallas import tpu as pltpu
from jax.sharding import PartitionSpec as P

STEPS = 3
EPSILON = 1e-06
RESTART = 0.2

F32 = jnp.float32
BF16 = jnp.bfloat16
VMEM = pl.BlockSpec(memory_space=pltpu.VMEM)
SMEM = pl.BlockSpec(memory_space=pltpu.SMEM)
EMPTY = 1024
COLUMNS = 8
SLOTS_OF = 64
META = 128
BACK = BF16
CHUNK = 2
KEPT = 3
EXTRA = 16


def nn(a, b):
    return lax.dot_general(a, b, (((1,), (0,)), ((), ())), preferred_element_type=F32)


def nt(a, b):
    return lax.dot_general(a, b, (((1,), (1,)), ((), ())), preferred_element_type=F32)


def call(kernel, outs, ins, out_specs=None, scratch=(), flops=1e6, moved=1e6, limit=16 * 1024 * 1024):
    return pl.pallas_call(
        kernel,
        out_shape=outs,
        in_specs=ins,
        out_specs=out_specs if out_specs is not None else jax.tree.map(lambda _: VMEM, outs),
        scratch_shapes=list(scratch),
        compiler_params=pltpu.CompilerParams(vmem_limit_bytes=limit),
        cost_estimate=pl.CostEstimate(
            flops=int(flops), bytes_accessed=int(moved), transcendentals=0
        ),
    )


def to_rows(first, second):
    cells = first.shape[0]
    lane = lax.broadcasted_iota(jnp.int32, (cells, 128), 1)
    wide = jnp.where(lane == 0, first, jnp.where(lane == 1, second, 0.0))
    wide = jnp.concatenate([wide, jnp.zeros((128 - cells, 128), F32)], axis=0)
    return wide.T[:8]


def to_columns(block, cells):
    wide = jnp.concatenate([block, jnp.zeros((120, 128), F32)], axis=0).T
    return wide[:cells, 0:1], wide[:cells, 1:2]


def degree_kernel(
    place, columns, counts, tiles, message, meta, near, row_sums, col_sums, used, done
):
    panels, slots, tile = tiles.shape[0], tiles.shape[1], tiles.shape[2]
    row_devices = message.shape[0]
    keeping = pltpu.make_async_copy(tiles.at[: near.shape[0]], near, done)
    keeping.start()
    mine_row, mine_col = place[0], place[1]
    meta[0] = mine_row
    meta[1] = mine_col
    for b in range(row_devices):
        used[b] = 0
    for i in range(panels):
        for s in range(slots):
            q = i * slots + s
            b = columns[i, 0, s]
            dead = jnp.where(s < counts[i, 0], 0, EMPTY)
            meta[COLUMNS + q] = b + dead
            meta[SLOTS_OF + 2 * b + used[b]] = q + dead
            used[b] = used[b] + 1

    ones = jnp.ones((16, tile), BF16)
    for i in range(panels):
        total = jnp.zeros((16, tile), F32)
        for s in range(slots):
            live = s < counts[i, 0]
            weight = jnp.where(live, ones, jnp.zeros_like(ones))
            value = tiles[i, s]
            total = total + nt(weight, value)
            wide = jnp.sum(value.astype(F32).reshape(tile // 8, 8, tile), axis=0)
            col_sums[i * slots + s] = jnp.where(live, wide, jnp.zeros_like(wide))
        row_sums[i : i + 1, :] = total[:1]
    rows = row_sums[...]
    everything = jnp.sum(jnp.sum(rows, axis=1, keepdims=True), axis=0, keepdims=True)
    for b in range(row_devices):
        first = meta[SLOTS_OF + 2 * b] % EMPTY
        second = meta[SLOTS_OF + 2 * b + 1] % EMPTY
        part = jnp.sum(col_sums[first] + col_sums[second], axis=0, keepdims=True)
        part = jnp.broadcast_to(part, rows.shape)
        at = lax.broadcasted_iota(jnp.int32, part.shape, 0)
        part = jnp.where(at == mine_col, part, 0.0) + jnp.where(b == mine_row, rows, 0.0)
        message[b, :, :tile] = part
        message[b, :, tile:] = jnp.broadcast_to(everything, (part.shape[0], 128))
    keeping.wait()


def pack(values, dots, many, one):
    cells = values.shape[0]
    body = values.astype(BF16)
    high = dots.astype(BF16)
    low = (dots - high.astype(F32)).astype(BF16)
    tail = jnp.concatenate([high, low], axis=0)
    tail = jnp.concatenate([tail, jnp.zeros_like(tail)], axis=1)
    one[...] = body
    for b in range(many.shape[0]):
        many[b, :cells] = body
        many[b, cells:] = tail


def start_kernel(total_cells, parts, start, degrees, scales, many, one):
    tile = start.shape[1]
    sums = jnp.sum(parts[...], axis=0, keepdims=True)
    degree = sums[:, :tile]
    volume = 2.0 * sums[:, tile : tile + 1]
    inv_root = 1.0 / jnp.sqrt(degree + volume / total_cells)
    leading = jnp.sqrt(degree / volume)
    degrees[...] = degree
    scales[0:1, :] = inv_root
    scales[1:2, :] = leading
    wide = start[...].astype(F32)
    dot = jnp.sum(wide * leading, axis=1, keepdims=True)
    pack(wide * inv_root, to_rows(dot, jnp.zeros_like(dot)), many, one)


def product_kernel(
    meta, near_tiles, stored, gathered, own, pair, far1, far3, far2, result, keep, give,
    buffer, parts, far_tiles, arrived,
):
    split, slots = near_tiles.shape[0], near_tiles.shape[1]
    panels = stored.shape[0]
    cells = own.shape[0]
    fetch = {}
    for first in range(split, panels, CHUNK):
        last = min(first + CHUNK, panels)
        fetch[first] = pltpu.make_async_copy(
            stored.at[first:last],
            far_tiles.at[first - split : last - split],
            arrived.at[(first - split) // CHUNK],
        )
        fetch[first].start()
    zs = panels // 2
    z, core = meta[1] // 2, meta[1] % 2
    dots = jnp.zeros((8, 128), F32)
    for b in range(gathered.shape[0]):
        tail = gathered[b, cells:, :128].astype(F32)
        dots = dots + tail[:8] + tail[8:]
    dots = jnp.concatenate([dots, jnp.zeros_like(dots)], axis=1)
    for k, source in ((0, None), (1, far1), (2, far2), (3, far3)):
        at = (z + zs - k) % zs
        same = own[...] if source is None else source[0]
        other = pair[...] if source is None else source[1]
        buffer[2 * at + core] = same
        buffer[2 * at + 1 - core] = other
    for at in range(zs):
        k = (at + zs - z) % zs
        totals = []
        for i in (2 * at, 2 * at + 1):
            if i in fetch:
                fetch[i].wait()
            tiles, row = (near_tiles, i) if i < split else (far_tiles, i - split)
            mine = buffer[i]
            total = None
            for s in range(slots):
                held = meta[COLUMNS + i * slots + s]
                panel = gathered[held % EMPTY, :cells]
                panel = jnp.where(held < EMPTY, panel, jnp.zeros_like(panel))
                part = nt(panel, tiles[row, s])
                total = part if total is None else total + part
                parts[i * slots + s] = nn(mine, tiles[row, s])
            totals.append(total)
        keep[k, :cells] = jnp.where(core == 0, totals[0], totals[1])
        give[k, :cells] = jnp.where(core == 0, totals[1], totals[0])
        keep[k, cells:] = dots
        give[k, cells:] = dots
    for b in range(result.shape[0]):
        total = None
        for m in range(2):
            held = meta[SLOTS_OF + 2 * b + m]
            part = parts[held % EMPTY]
            part = jnp.where(held < EMPTY, part, jnp.zeros_like(part))
            total = part if total is None else total + part
        result[b] = total.astype(result.dtype)


def gather_sums(tile_sums, near, far1, far3, far2, scales, cells):
    total = tile_sums[0].astype(F32)
    for b in range(1, tile_sums.shape[0]):
        total = total + tile_sums[b].astype(F32)
    side = near[...] + far1[...] + far2[...] + far3[...]
    product = (total + side[:cells]) * scales[0:1, :]
    return product, side[cells:, :128]


def first_kernel(tile_sums, near, far1, far3, far2, scales, many, one, applied, dots0, residual):
    cells = applied.shape[0]
    product, side = gather_sums(tile_sums, near, far1, far3, far2, scales, cells)
    projection, _ = to_columns(side, cells)
    applied[...] = product
    dots0[...] = side
    finish(product, projection, scales, many, one, residual)


def finish(applied, projection, scales, many, one, residual):
    inv_root, leading = scales[0:1, :], scales[1:2, :]
    rest = applied - projection * leading
    residual[...] = rest
    norm = jnp.sum(rest * rest, axis=1, keepdims=True)
    dot = jnp.sum(rest * leading, axis=1, keepdims=True)
    pack(rest * inv_root, to_rows(norm, dot), many, one)


def next_applied(total_cells, product, side, applied0, dots0, cells):
    norm, dot = to_columns(side, cells)
    start_dot, _ = to_columns(dots0[...], cells)
    scale = (1.0 - RESTART) / jnp.sqrt(norm / total_cells + EPSILON)
    applied = scale * product + RESTART * applied0[...]
    return applied, scale * dot + RESTART * start_dot


def middle_kernel(
    total_cells, tile_sums, near, far1, far3, far2, scales, applied0, dots0, many, one, residual
):
    cells = applied0.shape[0]
    product, side = gather_sums(tile_sums, near, far1, far3, far2, scales, cells)
    applied, projection = next_applied(total_cells, product, side, applied0, dots0, cells)
    finish(applied, projection, scales, many, one, residual)


def last_kernel(
    total_cells, tile_sums, near, far1, far3, far2, scales, applied0, dots0, norms, residual
):
    cells = applied0.shape[0]
    product, side = gather_sums(tile_sums, near, far1, far3, far2, scales, cells)
    applied, projection = next_applied(total_cells, product, side, applied0, dots0, cells)
    rest = applied - projection * scales[1:2, :]
    residual[...] = rest
    norm = jnp.sum(rest * rest, axis=1, keepdims=True)
    norms[...] = jnp.broadcast_to(to_rows(norm, norm)[:1], norms.shape)


def blend_kernel(total_cells, norms, residual, start, embedding):
    cells = start.shape[0]
    row = jnp.sum(norms[...], axis=0, keepdims=True)
    norm, _ = to_columns(jnp.concatenate([row, jnp.zeros((7, 128), F32)], axis=0), cells)
    scaled = residual[...] / jnp.sqrt(norm / total_cells + EPSILON)
    embedding[...] = (1.0 - RESTART) * scaled + RESTART * start[...].astype(F32)


def local(tile_values, tile_cols, row_counts, start_basis):
    rows, cols = lax.axis_size("row"), lax.axis_size("col")
    panels, _, slots, tile, _ = tile_values.shape
    cells = start_basis.shape[0]
    zs = cols // 2
    total_cells = rows * cols * tile
    tiles = tile_values.reshape(panels, slots, tile, tile)
    stored = pltpu.with_memory_space_constraint(tiles, pltpu.HBM)
    place = jnp.stack([lax.axis_index("row"), lax.axis_index("col")]).astype(jnp.int32)
    shape = jax.ShapeDtypeStruct
    swap = [(i, i ^ 1) for i in range(cols)]
    shift = lambda k: [(i, (i + 2 * k) % cols) for i in range(cols)]
    tile_bytes = panels * slots * tile * tile * 2
    work = 2 * panels * slots * cells * tile * tile

    message, meta, near_tiles = call(
        degree_kernel,
        (
            shape((rows, cols, tile + 128), F32),
            shape((META,), jnp.int32),
            shape((KEPT, slots, tile, tile), BF16),
        ),
        [SMEM, SMEM, SMEM, VMEM],
        (VMEM, SMEM, VMEM),
        [
            pltpu.VMEM((panels, tile), F32),
            pltpu.VMEM((panels * slots, 8, tile), F32),
            pltpu.SMEM((rows,), jnp.int32),
            pltpu.SemaphoreType.DMA,
        ],
        work / 4,
        tile_bytes,
    )(place, tile_cols, row_counts, tiles)
    parts = lax.all_to_all(
        message.reshape(rows * cols, tile + 128), ("row", "col"), 0, 0, tiled=True
    )

    many_shape = shape((rows, cells + EXTRA, tile), BF16)
    one_shape = shape((cells, tile), BF16)
    full = shape((cells, tile), F32)
    degrees, scales, many, one = call(
        lambda *refs: start_kernel(total_cells, *refs),
        (shape((1, tile), F32), shape((8, tile), F32), many_shape, one_shape),
        [VMEM, VMEM],
    )(parts, start_basis)

    applied0 = dots0 = residual = None
    for step in range(STEPS):
        pair = lax.ppermute(one, "col", swap)
        both = jnp.stack([one, pair])
        near = [lax.ppermute(both, "col", shift(k)) for k in (1, 3, 2)]
        gathered = lax.all_to_all(many, "row", 0, 0, tiled=True)
        side_shape = shape((zs, cells + 8, tile), F32)
        back, keep, give = call(
            product_kernel,
            (shape((rows, cells, tile), BACK), side_shape, side_shape),
            [SMEM, VMEM, pl.BlockSpec(memory_space=pltpu.HBM)] + [VMEM] * 6,
            scratch=[
                pltpu.VMEM((panels, cells, tile), BF16),
                pltpu.VMEM((panels * slots, cells, tile), F32),
                pltpu.VMEM((panels - KEPT, slots, tile, tile), BF16),
                pltpu.SemaphoreType.DMA((pl.cdiv(panels - KEPT, CHUNK),)),
            ],
            flops=2 * work,
            moved=tile_bytes,
        )(meta, near_tiles, stored, gathered, one, pair, *near)
        back = lax.all_to_all(back, "row", 0, 0, tiled=True)
        given = lax.ppermute(give, "col", swap)
        sums = keep + given
        sides = [sums[0]] + [lax.ppermute(sums[k], "col", shift(k)) for k in (1, 3, 2)]
        arrived = (back, *sides, scales)
        if step == 0:
            many, one, applied0, dots0, residual = call(
                first_kernel,
                (many_shape, one_shape, full, shape((8, 128), F32), full),
                [VMEM] * 6,
            )(*arrived)
        elif step + 1 < STEPS:
            many, one, residual = call(
                lambda *refs: middle_kernel(total_cells, *refs),
                (many_shape, one_shape, full),
                [VMEM] * 8,
            )(*arrived, applied0, dots0)
        else:
            norms, residual = call(
                lambda *refs: last_kernel(total_cells, *refs),
                (shape((rows * cols, 128), F32), full),
                [VMEM] * 8,
            )(*arrived, applied0, dots0)
    norms = lax.all_to_all(norms, ("row", "col"), 0, 0, tiled=True)
    embedding = call(
        lambda *refs: blend_kernel(total_cells, *refs), full, [VMEM] * 3
    )(norms, residual, start_basis)
    return (embedding, degrees.reshape(tile))


def solution(mesh):
    placed = (
        P("row", "col", None, None, None),
        P("row", "col", None),
        P("row", "col"),
        P(None, ("row", "col")),
    )
    return jax.shard_map(
        local,
        mesh=mesh,
        in_specs=placed,
        out_specs=(P(None, ("row", "col")), P(("row", "col"))),
        check_vma=False,
    )
```

```python
import jax
import jax.numpy as jnp
from jax import lax
from jax.experimental import pallas as pl
from jax.experimental.pallas import tpu as pltpu
from jax.sharding import PartitionSpec as P

STEPS = 3
EPSILON = 1e-06
RESTART = 0.2

F32 = jnp.float32
BF16 = jnp.bfloat16
VMEM = pl.BlockSpec(memory_space=pltpu.VMEM)
SMEM = pl.BlockSpec(memory_space=pltpu.SMEM)
HBM = pl.BlockSpec(memory_space=pltpu.HBM)
EMPTY = 1024
COLUMNS = 8
SLOTS_OF = 64
META = 128
BACK = BF16
CHUNK = 2
KEPT = 3
EXTRA = 8


def in_hbm(x):
    return pltpu.with_memory_space_constraint(x, pltpu.HBM)


def nn(a, b):
    return lax.dot_general(a, b, (((1,), (0,)), ((), ())), preferred_element_type=F32)


def nt(a, b):
    return lax.dot_general(a, b, (((1,), (1,)), ((), ())), preferred_element_type=F32)


def call(kernel, outs, ins, out_specs=None, scratch=(), flops=1e6, moved=1e6, limit=16 * 1024 * 1024):
    return pl.pallas_call(
        kernel,
        out_shape=outs,
        in_specs=ins,
        out_specs=out_specs if out_specs is not None else jax.tree.map(lambda _: VMEM, outs),
        scratch_shapes=list(scratch),
        compiler_params=pltpu.CompilerParams(vmem_limit_bytes=limit),
        cost_estimate=pl.CostEstimate(
            flops=int(flops), bytes_accessed=int(moved), transcendentals=0
        ),
    )


def to_rows(first, second):
    cells = first.shape[0]
    lane = lax.broadcasted_iota(jnp.int32, (cells, 128), 1)
    wide = jnp.where(lane == 0, first, jnp.where(lane == 1, second, 0.0))
    wide = jnp.concatenate([wide, jnp.zeros((128 - cells, 128), F32)], axis=0)
    return wide.T[:8]


def to_columns(block, cells):
    wide = jnp.concatenate([block, jnp.zeros((120, 128), F32)], axis=0).T
    return wide[:cells, 0:1], wide[:cells, 1:2]


def degree_kernel(
    place, stored_columns, stored_counts, stored, message, meta, near,
    far, columns, counts, row_sums, col_sums, used, few, arrived,
):
    panels, slots, tile = stored.shape[0], stored.shape[1], stored.shape[2]
    row_devices = message.shape[0]
    split = near.shape[0]
    small = [
        pltpu.make_async_copy(stored_columns, columns, few.at[0]),
        pltpu.make_async_copy(stored_counts, counts, few.at[1]),
    ]
    for copy in small:
        copy.start()
    fetch = []
    for i in range(panels):
        held = near.at[i] if i < split else far.at[i - split]
        fetch.append(pltpu.make_async_copy(stored.at[i], held, arrived.at[i]))
        fetch[i].start()
    for copy in small:
        copy.wait()
    mine_row, mine_col = place[0], place[1]
    meta[0] = mine_row
    meta[1] = mine_col
    for b in range(row_devices):
        used[b] = 0
    for i in range(panels):
        for s in range(slots):
            q = i * slots + s
            b = columns[s, i]
            dead = jnp.where(s < counts[0, i], 0, EMPTY)
            meta[COLUMNS + q] = b + dead
            meta[SLOTS_OF + 2 * b + used[b]] = q + dead
            used[b] = used[b] + 1

    ones = jnp.ones((16, tile), BF16)
    for i in range(panels):
        if i % 2 == 0:
            fetch[i].wait()
            fetch[i + 1].wait()
        total = jnp.zeros((16, tile), F32)
        for s in range(slots):
            live = s < counts[0, i]
            weight = jnp.where(live, ones, jnp.zeros_like(ones))
            value = near[i, s] if i < split else far[i - split, s]
            total = total + nt(weight, value)
            wide = jnp.sum(value.astype(F32).reshape(tile // 8, 8, tile), axis=0)
            col_sums[i * slots + s] = jnp.where(live, wide, jnp.zeros_like(wide))
        row_sums[i : i + 1, :] = total[:1]
    rows = row_sums[...]
    everything = jnp.sum(jnp.sum(rows, axis=1, keepdims=True), axis=0, keepdims=True)
    for b in range(row_devices):
        first = meta[SLOTS_OF + 2 * b] % EMPTY
        second = meta[SLOTS_OF + 2 * b + 1] % EMPTY
        part = jnp.sum(col_sums[first] + col_sums[second], axis=0, keepdims=True)
        part = jnp.broadcast_to(part, rows.shape)
        at = lax.broadcasted_iota(jnp.int32, part.shape, 0)
        part = jnp.where(at == mine_col, part, 0.0) + jnp.where(b == mine_row, rows, 0.0)
        message[b, :, :tile] = part
        message[b, :, tile:] = jnp.broadcast_to(everything, (part.shape[0], 128))


def pack(values, dots, many, one):
    cells = values.shape[0]
    body = values.astype(BF16)
    high = dots.astype(BF16)
    low = (dots - high.astype(F32)).astype(BF16)
    tail = jnp.concatenate([high, low], axis=1)
    one[...] = body
    for b in range(many.shape[0]):
        many[b, :cells] = body
        many[b, cells:] = tail


def start_kernel(total_cells, parts, start, degrees, scales, many, one):
    tile = start.shape[1]
    sums = jnp.sum(parts[...], axis=0, keepdims=True)
    degree = sums[:, :tile]
    volume = 2.0 * sums[:, tile : tile + 1]
    inv_root = 1.0 / jnp.sqrt(degree + volume / total_cells)
    leading = jnp.sqrt(degree / volume)
    degrees[...] = degree
    scales[0:1, :] = inv_root
    scales[1:2, :] = leading
    wide = start[...].astype(F32)
    dot = jnp.sum(wide * leading, axis=1, keepdims=True)
    pack(wide * inv_root, to_rows(dot, jnp.zeros_like(dot)), many, one)


def product_kernel(
    meta, near_tiles, stored, gathered, own, pair, far1, far3, far2, result, keep, give,
    buffer, parts, far_tiles, arrived,
):
    split, slots = near_tiles.shape[0], near_tiles.shape[1]
    panels = stored.shape[0]
    cells = own.shape[0]
    fetch = {}
    for first in range(split, panels, CHUNK):
        last = min(first + CHUNK, panels)
        fetch[first] = pltpu.make_async_copy(
            stored.at[first:last],
            far_tiles.at[first - split : last - split],
            arrived.at[(first - split) // CHUNK],
        )
        fetch[first].start()
    zs = panels // 2
    z, core = meta[1] // 2, meta[1] % 2
    dots = jnp.zeros((8, 128), F32)
    for b in range(gathered.shape[0]):
        tail = gathered[b, cells:].astype(F32)
        dots = dots + tail[:, :128] + tail[:, 128:]
    dots = jnp.concatenate([dots, jnp.zeros_like(dots)], axis=1)
    for k, source in ((0, None), (1, far1), (2, far2), (3, far3)):
        at = (z + zs - k) % zs
        same = own[...] if source is None else source[0]
        other = pair[...] if source is None else source[1]
        buffer[2 * at + core] = same
        buffer[2 * at + 1 - core] = other
    for at in range(zs):
        k = (at + zs - z) % zs
        totals = []
        for i in (2 * at, 2 * at + 1):
            if i in fetch:
                fetch[i].wait()
            tiles, row = (near_tiles, i) if i < split else (far_tiles, i - split)
            mine = buffer[i]
            total = None
            for s in range(slots):
                held = meta[COLUMNS + i * slots + s]
                panel = gathered[held % EMPTY, :cells]
                panel = jnp.where(held < EMPTY, panel, jnp.zeros_like(panel))
                part = nt(panel, tiles[row, s])
                total = part if total is None else total + part
                parts[i * slots + s] = nn(mine, tiles[row, s])
            totals.append(total)
        keep[k, :cells] = jnp.where(core == 0, totals[0], totals[1])
        give[k, :cells] = jnp.where(core == 0, totals[1], totals[0])
        keep[k, cells:] = dots
        give[k, cells:] = dots
    for b in range(result.shape[0]):
        total = None
        for m in range(2):
            held = meta[SLOTS_OF + 2 * b + m]
            part = parts[held % EMPTY]
            part = jnp.where(held < EMPTY, part, jnp.zeros_like(part))
            total = part if total is None else total + part
        result[b] = total.astype(result.dtype)


def gather_sums(tile_sums, near, far1, far3, far2, scales, cells):
    total = tile_sums[0].astype(F32)
    for b in range(1, tile_sums.shape[0]):
        total = total + tile_sums[b].astype(F32)
    side = near[...] + far1[...] + far2[...] + far3[...]
    product = (total + side[:cells]) * scales[0:1, :]
    return product, side[cells:, :128]


def first_kernel(tile_sums, near, far1, far3, far2, scales, many, one, applied, dots0, residual):
    cells = applied.shape[0]
    product, side = gather_sums(tile_sums, near, far1, far3, far2, scales, cells)
    projection, _ = to_columns(side, cells)
    applied[...] = product
    dots0[...] = side
    finish(product, projection, scales, many, one, residual)


def finish(applied, projection, scales, many, one, residual):
    inv_root, leading = scales[0:1, :], scales[1:2, :]
    rest = applied - projection * leading
    residual[...] = rest
    norm = jnp.sum(rest * rest, axis=1, keepdims=True)
    dot = jnp.sum(rest * leading, axis=1, keepdims=True)
    pack(rest * inv_root, to_rows(norm, dot), many, one)


def next_applied(total_cells, product, side, applied0, dots0, cells):
    norm, dot = to_columns(side, cells)
    start_dot, _ = to_columns(dots0[...], cells)
    scale = (1.0 - RESTART) / jnp.sqrt(norm / total_cells + EPSILON)
    applied = scale * product + RESTART * applied0[...]
    return applied, scale * dot + RESTART * start_dot


def middle_kernel(
    total_cells, tile_sums, near, far1, far3, far2, scales, applied0, dots0, many, one, residual
):
    cells = applied0.shape[0]
    product, side = gather_sums(tile_sums, near, far1, far3, far2, scales, cells)
    applied, projection = next_applied(total_cells, product, side, applied0, dots0, cells)
    finish(applied, projection, scales, many, one, residual)


def last_kernel(
    total_cells, tile_sums, near, far1, far3, far2, scales, applied0, dots0, norms, residual
):
    cells = applied0.shape[0]
    product, side = gather_sums(tile_sums, near, far1, far3, far2, scales, cells)
    applied, projection = next_applied(total_cells, product, side, applied0, dots0, cells)
    rest = applied - projection * scales[1:2, :]
    residual[...] = rest
    norm = jnp.sum(rest * rest, axis=1, keepdims=True)
    norms[...] = jnp.broadcast_to(to_rows(norm, norm)[:1], norms.shape)


def blend_kernel(total_cells, norms, residual, start, embedding):
    cells = start.shape[0]
    row = jnp.sum(norms[...], axis=0, keepdims=True)
    norm, _ = to_columns(jnp.concatenate([row, jnp.zeros((7, 128), F32)], axis=0), cells)
    scaled = residual[...] / jnp.sqrt(norm / total_cells + EPSILON)
    embedding[...] = (1.0 - RESTART) * scaled + RESTART * start[...].astype(F32)


def local(tile_values, tile_cols, row_counts, start_basis):
    rows, cols = lax.axis_size("row"), lax.axis_size("col")
    panels, _, slots, tile, _ = tile_values.shape
    cells = start_basis.shape[0]
    zs = cols // 2
    total_cells = rows * cols * tile
    tiles = tile_values.reshape(panels, slots, tile, tile)
    stored = in_hbm(tiles)
    place = jnp.stack([lax.axis_index("row"), lax.axis_index("col")]).astype(jnp.int32)
    shape = jax.ShapeDtypeStruct
    swap = [(i, i ^ 1) for i in range(cols)]
    shift = lambda k: [(i, (i + 2 * k) % cols) for i in range(cols)]
    tile_bytes = panels * slots * tile * tile * 2
    work = 2 * panels * slots * cells * tile * tile

    message, meta, near_tiles = call(
        degree_kernel,
        (
            shape((rows, cols, tile + 128), F32),
            shape((META,), jnp.int32),
            shape((KEPT, slots, tile, tile), BF16),
        ),
        [SMEM, HBM, HBM, HBM],
        (VMEM, SMEM, VMEM),
        [
            pltpu.VMEM((panels - KEPT, slots, tile, tile), BF16),
            pltpu.SMEM((slots, panels), jnp.int32),
            pltpu.SMEM((1, panels), jnp.int32),
            pltpu.VMEM((panels, tile), F32),
            pltpu.VMEM((panels * slots, 8, tile), F32),
            pltpu.SMEM((rows,), jnp.int32),
            pltpu.SemaphoreType.DMA((2,)),
            pltpu.SemaphoreType.DMA((panels,)),
        ],
        work / 4,
        tile_bytes,
    )(place, in_hbm(tile_cols[:, 0].T), in_hbm(row_counts.T), stored)
    parts = lax.all_to_all(
        message.reshape(rows * cols, tile + 128), ("row", "col"), 0, 0, tiled=True
    )

    many_shape = shape((rows, cells + EXTRA, tile), BF16)
    one_shape = shape((cells, tile), BF16)
    full = shape((cells, tile), F32)
    degrees, scales, many, one = call(
        lambda *refs: start_kernel(total_cells, *refs),
        (shape((1, tile), F32), shape((8, tile), F32), many_shape, one_shape),
        [VMEM, VMEM],
    )(parts, start_basis)

    applied0 = dots0 = residual = None
    for step in range(STEPS):
        pair = lax.ppermute(one, "col", swap)
        both = jnp.stack([one, pair])
        near = [lax.ppermute(both, "col", shift(k)) for k in (1, 3, 2)]
        gathered = lax.all_to_all(many, "row", 0, 0, tiled=True)
        side_shape = shape((zs, cells + 8, tile), F32)
        back, keep, give = call(
            product_kernel,
            (shape((rows, cells, tile), BACK), side_shape, side_shape),
            [SMEM, VMEM, HBM] + [VMEM] * 6,
            scratch=[
                pltpu.VMEM((panels, cells, tile), BF16),
                pltpu.VMEM((panels * slots, cells, tile), F32),
                pltpu.VMEM((panels - KEPT, slots, tile, tile), BF16),
                pltpu.SemaphoreType.DMA((pl.cdiv(panels - KEPT, CHUNK),)),
            ],
            flops=2 * work,
            moved=tile_bytes,
        )(meta, near_tiles, stored, gathered, one, pair, *near)
        back = lax.all_to_all(back, "row", 0, 0, tiled=True)
        given = lax.ppermute(give, "col", swap)
        sums = keep + given
        sides = [sums[0]] + [lax.ppermute(sums[k], "col", shift(k)) for k in (1, 3, 2)]
        arrived = (back, *sides, scales)
        if step == 0:
            many, one, applied0, dots0, residual = call(
                first_kernel,
                (many_shape, one_shape, full, shape((8, 128), F32), full),
                [VMEM] * 6,
            )(*arrived)
        elif step + 1 < STEPS:
            many, one, residual = call(
                lambda *refs: middle_kernel(total_cells, *refs),
                (many_shape, one_shape, full),
                [VMEM] * 8,
            )(*arrived, applied0, dots0)
        else:
            norms, residual = call(
                lambda *refs: last_kernel(total_cells, *refs),
                (shape((rows * cols, 128), F32), full),
                [VMEM] * 8,
            )(*arrived, applied0, dots0)
    norms = lax.all_to_all(norms, ("row", "col"), 0, 0, tiled=True)
    embedding = call(
        lambda *refs: blend_kernel(total_cells, *refs), full, [VMEM] * 3
    )(norms, residual, start_basis)
    return (embedding, degrees.reshape(tile))


def solution(mesh):
    placed = (
        P("row", "col", None, None, None),
        P("row", "col", None),
        P("row", "col"),
        P(None, ("row", "col")),
    )
    return jax.shard_map(
        local,
        mesh=mesh,
        in_specs=placed,
        out_specs=(P(None, ("row", "col")), P(("row", "col"))),
        check_vma=False,
    )
```

```python
import jax
import jax.numpy as jnp
from jax import lax
from jax.experimental import pallas as pl
from jax.experimental.pallas import tpu as pltpu
from jax.sharding import PartitionSpec as P

STEPS = 3
EPSILON = 1e-06
RESTART = 0.2

F32 = jnp.float32
BF16 = jnp.bfloat16
VMEM = pl.BlockSpec(memory_space=pltpu.VMEM)
SMEM = pl.BlockSpec(memory_space=pltpu.SMEM)
HBM = pl.BlockSpec(memory_space=pltpu.HBM)
EMPTY = 1024
COLUMNS = 8
SLOTS_OF = 64
META = 128
BACK = BF16
COUNTS = 40
KEPT = 6
FIRST = 2
EXTRA = 8


def in_hbm(x):
    return pltpu.with_memory_space_constraint(x, pltpu.HBM)


def nn(a, b):
    return lax.dot_general(a, b, (((1,), (0,)), ((), ())), preferred_element_type=F32)


def nt(a, b):
    return lax.dot_general(a, b, (((1,), (1,)), ((), ())), preferred_element_type=F32)


def call(kernel, outs, ins, out_specs=None, scratch=(), flops=1e6, moved=1e6, limit=16 * 1024 * 1024):
    return pl.pallas_call(
        kernel,
        out_shape=outs,
        in_specs=ins,
        out_specs=out_specs if out_specs is not None else jax.tree.map(lambda _: VMEM, outs),
        scratch_shapes=list(scratch),
        compiler_params=pltpu.CompilerParams(vmem_limit_bytes=limit),
        cost_estimate=pl.CostEstimate(
            flops=int(flops), bytes_accessed=int(moved), transcendentals=0
        ),
    )


def to_rows(first, second):
    cells = first.shape[0]
    lane = lax.broadcasted_iota(jnp.int32, (cells, 128), 1)
    wide = jnp.where(lane == 0, first, jnp.where(lane == 1, second, 0.0))
    wide = jnp.concatenate([wide, jnp.zeros((128 - cells, 128), F32)], axis=0)
    return wide.T[:8]


def to_columns(block, cells):
    wide = jnp.concatenate([block, jnp.zeros((120, 128), F32)], axis=0).T
    return wide[:cells, 0:1], wide[:cells, 1:2]


def degree_kernel(
    place, stored_columns, stored_counts, stored, message, meta, near,
    far, columns, counts, row_sums, col_sums, used, few, arrived,
):
    panels, slots, tile = stored.shape[0], stored.shape[1], stored.shape[2]
    row_devices = message.shape[0]
    split, first = near.shape[0], near.shape[1]
    small = [
        pltpu.make_async_copy(stored_columns, columns, few.at[0]),
        pltpu.make_async_copy(stored_counts, counts, few.at[1]),
    ]
    for copy in small:
        copy.start()
    fetch = []
    for i in range(panels):
        for h, part in enumerate((pl.ds(0, first), pl.ds(first, slots - first))):
            held = near.at[i] if i < split and h == 0 else far.at[i, part]
            fetch.append(pltpu.make_async_copy(stored.at[i, part], held, arrived.at[i, h]))
    for copy in fetch:
        copy.start()
    for copy in small:
        copy.wait()
    mine_row, mine_col = place[0], place[1]
    meta[0] = mine_row
    meta[1] = mine_col
    for b in range(row_devices):
        used[b] = 0
    for i in range(panels):
        meta[COUNTS + i] = counts[0, i]
        for s in range(slots):
            q = i * slots + s
            b = columns[s, i]
            dead = jnp.where(s < counts[0, i], 0, EMPTY)
            meta[COLUMNS + q] = b + dead
            meta[SLOTS_OF + 2 * b + used[b]] = q + dead
            used[b] = used[b] + 1

    ones = jnp.ones((16, tile), BF16)
    for i in range(panels):
        if i % 2 == 0:
            for copy in fetch[2 * i : 2 * i + 4]:
                copy.wait()
        total = jnp.zeros((16, tile), F32)
        for s in range(slots):
            live = s < counts[0, i]
            weight = jnp.where(live, ones, jnp.zeros_like(ones))
            value = near[i, s] if i < split and s < first else far[i, s]
            total = total + nt(weight, value)
            wide = jnp.sum(value.astype(F32).reshape(tile // 8, 8, tile), axis=0)
            col_sums[i * slots + s] = jnp.where(live, wide, jnp.zeros_like(wide))
        row_sums[i : i + 1, :] = total[:1]
    rows = row_sums[...]
    everything = jnp.sum(jnp.sum(rows, axis=1, keepdims=True), axis=0, keepdims=True)
    for b in range(row_devices):
        first = meta[SLOTS_OF + 2 * b] % EMPTY
        second = meta[SLOTS_OF + 2 * b + 1] % EMPTY
        part = jnp.sum(col_sums[first] + col_sums[second], axis=0, keepdims=True)
        part = jnp.broadcast_to(part, rows.shape)
        at = lax.broadcasted_iota(jnp.int32, part.shape, 0)
        part = jnp.where(at == mine_col, part, 0.0) + jnp.where(b == mine_row, rows, 0.0)
        message[b, :, :tile] = part
        message[b, :, tile:] = jnp.broadcast_to(everything, (part.shape[0], 128))


def pack(values, dots, many, one):
    cells = values.shape[0]
    body = values.astype(BF16)
    high = dots.astype(BF16)
    low = (dots - high.astype(F32)).astype(BF16)
    tail = jnp.concatenate([high, low], axis=1)
    one[...] = body
    for b in range(many.shape[0]):
        many[b, :cells] = body
        many[b, cells:] = tail


def start_kernel(total_cells, parts, start, degrees, scales, many, one):
    tile = start.shape[1]
    sums = jnp.sum(parts[...], axis=0, keepdims=True)
    degree = sums[:, :tile]
    volume = 2.0 * sums[:, tile : tile + 1]
    inv_root = 1.0 / jnp.sqrt(degree + volume / total_cells)
    leading = jnp.sqrt(degree / volume)
    degrees[...] = degree
    scales[0:1, :] = inv_root
    scales[1:2, :] = leading
    wide = start[...].astype(F32)
    dot = jnp.sum(wide * leading, axis=1, keepdims=True)
    pack(wide * inv_root, to_rows(dot, jnp.zeros_like(dot)), many, one)


def product_kernel(
    meta, near_tiles, stored, gathered, own, pair, far1, far3, far2, result, keep, give,
    buffer, parts, totals, far_tiles, late_tiles, arrived, late,
):
    split, first = near_tiles.shape[0], near_tiles.shape[1]
    panels, slots = stored.shape[0], stored.shape[1]
    cells = own.shape[0]
    zs = panels // 2
    z, core = meta[1] // 2, meta[1] % 2
    fetch = []
    for i in range(split, panels):
        fetch.append(
            pltpu.make_async_copy(
                stored.at[i, pl.ds(0, first)], far_tiles.at[i - split], arrived.at[i - split]
            )
        )
        fetch[-1].start()
    later = []
    for i in range(panels):
        later.append(
            pltpu.make_async_copy(
                stored.at[i, pl.ds(first, slots - first)], late_tiles.at[i], late.at[i]
            )
        )
        pl.when(meta[COUNTS + i] > first)(later[i].start)
    dots = jnp.zeros((8, 128), F32)
    for b in range(gathered.shape[0]):
        tail = gathered[b, cells:].astype(F32)
        dots = dots + tail[:, :128] + tail[:, 128:]
    dots = jnp.concatenate([dots, jnp.zeros_like(dots)], axis=1)
    for k, source in ((0, None), (1, far1), (2, far2), (3, far3)):
        at = (z + zs - k) % zs
        same = own[...] if source is None else source[0]
        other = pair[...] if source is None else source[1]
        buffer[2 * at + core] = same
        buffer[2 * at + 1 - core] = other

    def multiply(i, s, value):
        held = meta[COLUMNS + i * slots + s]
        panel = gathered[held % EMPTY, :cells]
        panel = jnp.where(held < EMPTY, panel, jnp.zeros_like(panel))
        parts[i * slots + s] = nn(buffer[i], value)
        return nt(panel, value)

    for i in range(panels):
        if i == split:
            for copy in fetch:
                copy.wait()
        total = None
        for s in range(first):
            value = near_tiles[i, s] if i < split else far_tiles[i - split, s]
            part = multiply(i, s, value)
            total = part if total is None else total + part
        totals[i] = total

    for i in range(panels):

        @pl.when(meta[COUNTS + i] > first)
        def _():
            later[i].wait()
            total = totals[i]
            for s in range(first, slots):
                total = total + multiply(i, s, late_tiles[i, s - first])
            totals[i] = total

    for k in range(zs):
        at = (z + k) % zs
        keep[k, :cells] = totals[2 * at + core]
        give[k, :cells] = totals[2 * at + 1 - core]
        keep[k, cells:] = dots
        give[k, cells:] = dots
    for b in range(result.shape[0]):
        total = None
        for m in range(2):
            held = meta[SLOTS_OF + 2 * b + m]
            part = parts[held % EMPTY]
            part = jnp.where(held < EMPTY, part, jnp.zeros_like(part))
            total = part if total is None else total + part
        result[b] = total.astype(result.dtype)


def gather_sums(tile_sums, near, far1, far3, far2, scales, cells):
    total = tile_sums[0].astype(F32)
    for b in range(1, tile_sums.shape[0]):
        total = total + tile_sums[b].astype(F32)
    side = near[...] + far1[...] + far2[...] + far3[...]
    product = (total + side[:cells]) * scales[0:1, :]
    return product, side[cells:, :128]


def first_kernel(tile_sums, near, far1, far3, far2, scales, many, one, applied, dots0, residual):
    cells = applied.shape[0]
    product, side = gather_sums(tile_sums, near, far1, far3, far2, scales, cells)
    projection, _ = to_columns(side, cells)
    applied[...] = product
    dots0[...] = side
    finish(product, projection, scales, many, one, residual)


def finish(applied, projection, scales, many, one, residual):
    inv_root, leading = scales[0:1, :], scales[1:2, :]
    rest = applied - projection * leading
    residual[...] = rest
    norm = jnp.sum(rest * rest, axis=1, keepdims=True)
    dot = jnp.sum(rest * leading, axis=1, keepdims=True)
    pack(rest * inv_root, to_rows(norm, dot), many, one)


def next_applied(total_cells, product, side, applied0, dots0, cells):
    norm, dot = to_columns(side, cells)
    start_dot, _ = to_columns(dots0[...], cells)
    scale = (1.0 - RESTART) / jnp.sqrt(norm / total_cells + EPSILON)
    applied = scale * product + RESTART * applied0[...]
    return applied, scale * dot + RESTART * start_dot


def middle_kernel(
    total_cells, tile_sums, near, far1, far3, far2, scales, applied0, dots0, many, one, residual
):
    cells = applied0.shape[0]
    product, side = gather_sums(tile_sums, near, far1, far3, far2, scales, cells)
    applied, projection = next_applied(total_cells, product, side, applied0, dots0, cells)
    finish(applied, projection, scales, many, one, residual)


def last_kernel(
    total_cells, tile_sums, near, far1, far3, far2, scales, applied0, dots0, norms, residual
):
    cells = applied0.shape[0]
    product, side = gather_sums(tile_sums, near, far1, far3, far2, scales, cells)
    applied, projection = next_applied(total_cells, product, side, applied0, dots0, cells)
    rest = applied - projection * scales[1:2, :]
    residual[...] = rest
    norm = jnp.sum(rest * rest, axis=1, keepdims=True)
    norms[...] = jnp.broadcast_to(to_rows(norm, norm)[:1], norms.shape)


def blend_kernel(total_cells, norms, residual, start, embedding):
    cells = start.shape[0]
    row = jnp.sum(norms[...], axis=0, keepdims=True)
    norm, _ = to_columns(jnp.concatenate([row, jnp.zeros((7, 128), F32)], axis=0), cells)
    scaled = residual[...] / jnp.sqrt(norm / total_cells + EPSILON)
    embedding[...] = (1.0 - RESTART) * scaled + RESTART * start[...].astype(F32)


def local(tile_values, tile_cols, row_counts, start_basis):
    rows, cols = lax.axis_size("row"), lax.axis_size("col")
    panels, _, slots, tile, _ = tile_values.shape
    cells = start_basis.shape[0]
    zs = cols // 2
    total_cells = rows * cols * tile
    tiles = tile_values.reshape(panels, slots, tile, tile)
    stored = in_hbm(tiles)
    place = jnp.stack([lax.axis_index("row"), lax.axis_index("col")]).astype(jnp.int32)
    shape = jax.ShapeDtypeStruct
    swap = [(i, i ^ 1) for i in range(cols)]
    shift = lambda k: [(i, (i + 2 * k) % cols) for i in range(cols)]
    tile_bytes = panels * slots * tile * tile * 2
    work = 2 * panels * slots * cells * tile * tile

    message, meta, near_tiles = call(
        degree_kernel,
        (
            shape((rows, cols, tile + 128), F32),
            shape((META,), jnp.int32),
            shape((KEPT, FIRST, tile, tile), BF16),
        ),
        [SMEM, HBM, HBM, HBM],
        (VMEM, SMEM, VMEM),
        [
            pltpu.VMEM(tiles.shape, BF16),
            pltpu.SMEM((slots, panels), jnp.int32),
            pltpu.SMEM((1, panels), jnp.int32),
            pltpu.VMEM((panels, tile), F32),
            pltpu.VMEM((panels * slots, 8, tile), F32),
            pltpu.SMEM((rows,), jnp.int32),
            pltpu.SemaphoreType.DMA((2,)),
            pltpu.SemaphoreType.DMA((panels, 2)),
        ],
        work / 4,
        tile_bytes,
    )(place, in_hbm(tile_cols[:, 0].T), in_hbm(row_counts.T), stored)
    parts = lax.all_to_all(
        message.reshape(rows * cols, tile + 128), ("row", "col"), 0, 0, tiled=True
    )

    many_shape = shape((rows, cells + EXTRA, tile), BF16)
    one_shape = shape((cells, tile), BF16)
    full = shape((cells, tile), F32)
    degrees, scales, many, one = call(
        lambda *refs: start_kernel(total_cells, *refs),
        (shape((1, tile), F32), shape((8, tile), F32), many_shape, one_shape),
        [VMEM, VMEM],
    )(parts, start_basis)

    applied0 = dots0 = residual = None
    for step in range(STEPS):
        pair = lax.ppermute(one, "col", swap)
        both = jnp.stack([one, pair])
        near = [lax.ppermute(both, "col", shift(k)) for k in (1, 3, 2)]
        gathered = lax.all_to_all(many, "row", 0, 0, tiled=True)
        side_shape = shape((zs, cells + 8, tile), F32)
        back, keep, give = call(
            product_kernel,
            (shape((rows, cells, tile), BACK), side_shape, side_shape),
            [SMEM, VMEM, HBM] + [VMEM] * 6,
            scratch=[
                pltpu.VMEM((panels, cells, tile), BF16),
                pltpu.VMEM((panels * slots, cells, tile), F32),
                pltpu.VMEM((panels, cells, tile), F32),
                pltpu.VMEM((panels - KEPT, FIRST, tile, tile), BF16),
                pltpu.VMEM((panels, slots - FIRST, tile, tile), BF16),
                pltpu.SemaphoreType.DMA((panels - KEPT,)),
                pltpu.SemaphoreType.DMA((panels,)),
            ],
            flops=2 * work,
            moved=tile_bytes,
        )(meta, near_tiles, stored, gathered, one, pair, *near)
        back = lax.all_to_all(back, "row", 0, 0, tiled=True)
        given = lax.ppermute(give, "col", swap)
        sums = keep + given
        sides = [sums[0]] + [lax.ppermute(sums[k], "col", shift(k)) for k in (1, 3, 2)]
        arrived = (back, *sides, scales)
        if step == 0:
            many, one, applied0, dots0, residual = call(
                first_kernel,
                (many_shape, one_shape, full, shape((8, 128), F32), full),
                [VMEM] * 6,
            )(*arrived)
        elif step + 1 < STEPS:
            many, one, residual = call(
                lambda *refs: middle_kernel(total_cells, *refs),
                (many_shape, one_shape, full),
                [VMEM] * 8,
            )(*arrived, applied0, dots0)
        else:
            norms, residual = call(
                lambda *refs: last_kernel(total_cells, *refs),
                (shape((rows * cols, 128), F32), full),
                [VMEM] * 8,
            )(*arrived, applied0, dots0)
    norms = lax.all_to_all(norms, ("row", "col"), 0, 0, tiled=True)
    embedding = call(
        lambda *refs: blend_kernel(total_cells, *refs), full, [VMEM] * 3
    )(norms, residual, start_basis)
    return (embedding, degrees.reshape(tile))


def solution(mesh):
    placed = (
        P("row", "col", None, None, None),
        P("row", "col", None),
        P("row", "col"),
        P(None, ("row", "col")),
    )
    return jax.shard_map(
        local,
        mesh=mesh,
        in_specs=placed,
        out_specs=(P(None, ("row", "col")), P(("row", "col"))),
        check_vma=False,
    )
```

```python
import jax
import jax.numpy as jnp
from jax import lax
from jax.experimental import pallas as pl
from jax.experimental.pallas import tpu as pltpu
from jax.sharding import PartitionSpec as P

STEPS = 3
EPSILON = 1e-06
RESTART = 0.2

F32 = jnp.float32
BF16 = jnp.bfloat16
VMEM = pl.BlockSpec(memory_space=pltpu.VMEM)
SMEM = pl.BlockSpec(memory_space=pltpu.SMEM)
HBM = pl.BlockSpec(memory_space=pltpu.HBM)
EMPTY = 1024
COLUMNS = 8
SLOTS_OF = 64
META = 128
BACK = BF16
COUNTS = 40
KEPT = 7
FIRST = 2
EXTRA = 8


def in_hbm(x):
    return pltpu.with_memory_space_constraint(x, pltpu.HBM)


def nn(a, b):
    return lax.dot_general(a, b, (((1,), (0,)), ((), ())), preferred_element_type=F32)


def nt(a, b):
    return lax.dot_general(a, b, (((1,), (1,)), ((), ())), preferred_element_type=F32)


def call(kernel, outs, ins, out_specs=None, scratch=(), flops=1e6, moved=1e6, limit=16 * 1024 * 1024):
    return pl.pallas_call(
        kernel,
        out_shape=outs,
        in_specs=ins,
        out_specs=out_specs if out_specs is not None else jax.tree.map(lambda _: VMEM, outs),
        scratch_shapes=list(scratch),
        compiler_params=pltpu.CompilerParams(vmem_limit_bytes=limit),
        cost_estimate=pl.CostEstimate(
            flops=int(flops), bytes_accessed=int(moved), transcendentals=0
        ),
    )


def to_rows(first, second):
    cells = first.shape[0]
    lane = lax.broadcasted_iota(jnp.int32, (cells, 128), 1)
    wide = jnp.where(lane == 0, first, jnp.where(lane == 1, second, 0.0))
    wide = jnp.concatenate([wide, jnp.zeros((128 - cells, 128), F32)], axis=0)
    return wide.T[:8]


def to_columns(block, cells):
    wide = jnp.concatenate([block, jnp.zeros((120, 128), F32)], axis=0).T
    return wide[:cells, 0:1], wide[:cells, 1:2]


def degree_kernel(
    place, stored_columns, stored_counts, stored, message, meta, near,
    far, columns, counts, row_sums, col_sums, used, few, arrived,
):
    panels, slots, tile = stored.shape[0], stored.shape[1], stored.shape[2]
    row_devices = message.shape[0]
    split, first = near.shape[0], near.shape[1]
    small = [
        pltpu.make_async_copy(stored_columns, columns, few.at[0]),
        pltpu.make_async_copy(stored_counts, counts, few.at[1]),
    ]
    for copy in small:
        copy.start()
    fetch = []
    for i in range(panels):
        for h, part in enumerate((pl.ds(0, first), pl.ds(first, slots - first))):
            held = near.at[i] if i < split and h == 0 else far.at[i, part]
            fetch.append(pltpu.make_async_copy(stored.at[i, part], held, arrived.at[i, h]))
    for copy in fetch:
        copy.start()
    for copy in small:
        copy.wait()
    mine_row, mine_col = place[0], place[1]
    meta[0] = mine_row
    meta[1] = mine_col
    for b in range(row_devices):
        used[b] = 0
    for i in range(panels):
        meta[COUNTS + i] = counts[0, i]
        for s in range(slots):
            q = i * slots + s
            b = columns[s, i]
            dead = jnp.where(s < counts[0, i], 0, EMPTY)
            meta[COLUMNS + q] = b + dead
            meta[SLOTS_OF + 2 * b + used[b]] = q + dead
            used[b] = used[b] + 1

    ones = jnp.ones((16, tile), BF16)
    for i in range(panels):
        if i % 2 == 0:
            for copy in fetch[2 * i : 2 * i + 4]:
                copy.wait()
        total = jnp.zeros((16, tile), F32)
        for s in range(slots):
            live = s < counts[0, i]
            weight = jnp.where(live, ones, jnp.zeros_like(ones))
            value = near[i, s] if i < split and s < first else far[i, s]
            total = total + nt(weight, value)
            wide = jnp.sum(value.astype(F32).reshape(tile // 8, 8, tile), axis=0)
            col_sums[i * slots + s] = jnp.where(live, wide, jnp.zeros_like(wide))
        row_sums[i : i + 1, :] = total[:1]
    rows = row_sums[...]
    everything = jnp.sum(jnp.sum(rows, axis=1, keepdims=True), axis=0, keepdims=True)
    for b in range(row_devices):
        first = meta[SLOTS_OF + 2 * b] % EMPTY
        second = meta[SLOTS_OF + 2 * b + 1] % EMPTY
        part = jnp.sum(col_sums[first] + col_sums[second], axis=0, keepdims=True)
        part = jnp.broadcast_to(part, rows.shape)
        at = lax.broadcasted_iota(jnp.int32, part.shape, 0)
        part = jnp.where(at == mine_col, part, 0.0) + jnp.where(b == mine_row, rows, 0.0)
        message[b, :, :tile] = part
        message[b, :, tile:] = jnp.broadcast_to(everything, (part.shape[0], 128))


def pack(values, dots, many, one):
    cells = values.shape[0]
    body = values.astype(BF16)
    high = dots.astype(BF16)
    low = (dots - high.astype(F32)).astype(BF16)
    tail = jnp.concatenate([high, low], axis=1)
    one[...] = body
    for b in range(many.shape[0]):
        many[b, :cells] = body
        many[b, cells:] = tail


def start_kernel(total_cells, parts, start, degrees, scales, many, one):
    tile = start.shape[1]
    sums = jnp.sum(parts[...], axis=0, keepdims=True)
    degree = sums[:, :tile]
    volume = 2.0 * sums[:, tile : tile + 1]
    inv_root = 1.0 / jnp.sqrt(degree + volume / total_cells)
    leading = jnp.sqrt(degree / volume)
    degrees[...] = degree
    scales[0:1, :] = inv_root
    scales[1:2, :] = leading
    wide = start[...].astype(F32)
    dot = jnp.sum(wide * leading, axis=1, keepdims=True)
    pack(wide * inv_root, to_rows(dot, jnp.zeros_like(dot)), many, one)


def product_kernel(
    meta, near_tiles, stored, gathered, own, pair, far1, far3, far2, result, keep, give,
    buffer, parts, totals, far_tiles, late_tiles, arrived, late,
):
    split, first = near_tiles.shape[0], near_tiles.shape[1]
    panels, slots = stored.shape[0], stored.shape[1]
    cells = own.shape[0]
    zs = panels // 2
    z, core = meta[1] // 2, meta[1] % 2
    fetch = []
    for i in range(split, panels):
        fetch.append(
            pltpu.make_async_copy(
                stored.at[i, pl.ds(0, first)], far_tiles.at[i - split], arrived.at[i - split]
            )
        )
        fetch[-1].start()
    later = []
    for i in range(panels):
        later.append(
            pltpu.make_async_copy(
                stored.at[i, pl.ds(first, slots - first)], late_tiles.at[i], late.at[i]
            )
        )
        pl.when(meta[COUNTS + i] > first)(later[i].start)
    dots = jnp.zeros((8, 128), F32)
    for b in range(gathered.shape[0]):
        tail = gathered[b, cells:].astype(F32)
        dots = dots + tail[:, :128] + tail[:, 128:]
    dots = jnp.concatenate([dots, jnp.zeros_like(dots)], axis=1)
    for k, source in ((0, None), (1, far1), (2, far2), (3, far3)):
        at = (z + zs - k) % zs
        same = own[...] if source is None else source[0]
        other = pair[...] if source is None else source[1]
        buffer[2 * at + core] = same
        buffer[2 * at + 1 - core] = other

    def multiply(i, s, value):
        held = meta[COLUMNS + i * slots + s]
        panel = gathered[held % EMPTY, :cells]
        panel = jnp.where(held < EMPTY, panel, jnp.zeros_like(panel))
        parts[i * slots + s] = nn(buffer[i], value)
        return nt(panel, value)

    for i in range(panels):
        if i == split:
            for copy in fetch:
                copy.wait()
        total = None
        for s in range(first):
            value = near_tiles[i, s] if i < split else far_tiles[i - split, s]
            part = multiply(i, s, value)
            total = part if total is None else total + part
        totals[i] = total

    for i in range(panels):

        @pl.when(meta[COUNTS + i] > first)
        def _():
            later[i].wait()
            total = totals[i]
            for s in range(first, slots):
                total = total + multiply(i, s, late_tiles[i, s - first])
            totals[i] = total

    for k in range(zs):
        at = (z + k) % zs
        keep[k, :cells] = totals[2 * at + core]
        give[k, :cells] = totals[2 * at + 1 - core]
        keep[k, cells:] = dots
        give[k, cells:] = dots
    for b in range(result.shape[0]):
        total = None
        for m in range(2):
            held = meta[SLOTS_OF + 2 * b + m]
            part = parts[held % EMPTY]
            part = jnp.where(held < EMPTY, part, jnp.zeros_like(part))
            total = part if total is None else total + part
        result[b] = total.astype(result.dtype)


def gather_sums(tile_sums, near, far1, far3, far2, scales, cells):
    total = tile_sums[0].astype(F32)
    for b in range(1, tile_sums.shape[0]):
        total = total + tile_sums[b].astype(F32)
    side = near[...] + far1[...] + far2[...] + far3[...]
    product = (total + side[:cells]) * scales[0:1, :]
    return product, side[cells:, :128]


def first_kernel(tile_sums, near, far1, far3, far2, scales, many, one, applied, dots0, residual):
    cells = applied.shape[0]
    product, side = gather_sums(tile_sums, near, far1, far3, far2, scales, cells)
    projection, _ = to_columns(side, cells)
    applied[...] = product
    dots0[...] = side
    finish(product, projection, scales, many, one, residual)


def finish(applied, projection, scales, many, one, residual):
    inv_root, leading = scales[0:1, :], scales[1:2, :]
    rest = applied - projection * leading
    residual[...] = rest
    norm = jnp.sum(rest * rest, axis=1, keepdims=True)
    dot = jnp.sum(rest * leading, axis=1, keepdims=True)
    pack(rest * inv_root, to_rows(norm, dot), many, one)


def next_applied(total_cells, product, side, applied0, dots0, cells):
    norm, dot = to_columns(side, cells)
    start_dot, _ = to_columns(dots0[...], cells)
    scale = (1.0 - RESTART) / jnp.sqrt(norm / total_cells + EPSILON)
    applied = scale * product + RESTART * applied0[...]
    return applied, scale * dot + RESTART * start_dot


def middle_kernel(
    total_cells, tile_sums, near, far1, far3, far2, scales, applied0, dots0, many, one, residual
):
    cells = applied0.shape[0]
    product, side = gather_sums(tile_sums, near, far1, far3, far2, scales, cells)
    applied, projection = next_applied(total_cells, product, side, applied0, dots0, cells)
    finish(applied, projection, scales, many, one, residual)


def last_kernel(
    total_cells, tile_sums, near, far1, far3, far2, scales, applied0, dots0, norms, residual
):
    cells = applied0.shape[0]
    product, side = gather_sums(tile_sums, near, far1, far3, far2, scales, cells)
    applied, projection = next_applied(total_cells, product, side, applied0, dots0, cells)
    rest = applied - projection * scales[1:2, :]
    residual[...] = rest
    norm = jnp.sum(rest * rest, axis=1, keepdims=True)
    norms[...] = jnp.broadcast_to(to_rows(norm, norm)[:1], norms.shape)


def blend_kernel(total_cells, norms, residual, start, embedding):
    cells = start.shape[0]
    row = jnp.sum(norms[...], axis=0, keepdims=True)
    norm, _ = to_columns(jnp.concatenate([row, jnp.zeros((7, 128), F32)], axis=0), cells)
    scaled = residual[...] / jnp.sqrt(norm / total_cells + EPSILON)
    embedding[...] = (1.0 - RESTART) * scaled + RESTART * start[...].astype(F32)


def local(tile_values, tile_cols, row_counts, start_basis):
    rows, cols = lax.axis_size("row"), lax.axis_size("col")
    panels, _, slots, tile, _ = tile_values.shape
    cells = start_basis.shape[0]
    zs = cols // 2
    total_cells = rows * cols * tile
    tiles = tile_values.reshape(panels, slots, tile, tile)
    stored = in_hbm(tiles)
    place = jnp.stack([lax.axis_index("row"), lax.axis_index("col")]).astype(jnp.int32)
    shape = jax.ShapeDtypeStruct
    swap = [(i, i ^ 1) for i in range(cols)]
    shift = lambda k: [(i, (i + 2 * k) % cols) for i in range(cols)]
    tile_bytes = panels * slots * tile * tile * 2
    work = 2 * panels * slots * cells * tile * tile

    message, meta, near_tiles = call(
        degree_kernel,
        (
            shape((rows, cols, tile + 128), F32),
            shape((META,), jnp.int32),
            shape((KEPT, FIRST, tile, tile), BF16),
        ),
        [SMEM, HBM, HBM, HBM],
        (VMEM, SMEM, VMEM),
        [
            pltpu.VMEM(tiles.shape, BF16),
            pltpu.SMEM((slots, panels), jnp.int32),
            pltpu.SMEM((1, panels), jnp.int32),
            pltpu.VMEM((panels, tile), F32),
            pltpu.VMEM((panels * slots, 8, tile), F32),
            pltpu.SMEM((rows,), jnp.int32),
            pltpu.SemaphoreType.DMA((2,)),
            pltpu.SemaphoreType.DMA((panels, 2)),
        ],
        work / 4,
        tile_bytes,
    )(place, in_hbm(tile_cols[:, 0].T), in_hbm(row_counts.T), stored)
    parts = lax.all_to_all(
        message.reshape(rows * cols, tile + 128), ("row", "col"), 0, 0, tiled=True
    )

    many_shape = shape((rows, cells + EXTRA, tile), BF16)
    one_shape = shape((cells, tile), BF16)
    full = shape((cells, tile), F32)
    degrees, scales, many, one = call(
        lambda *refs: start_kernel(total_cells, *refs),
        (shape((1, tile), F32), shape((8, tile), F32), many_shape, one_shape),
        [VMEM, VMEM],
    )(parts, start_basis)

    applied0 = dots0 = residual = None
    for step in range(STEPS):
        pair = lax.ppermute(one, "col", swap)
        both = jnp.stack([one, pair])
        near = [lax.ppermute(both, "col", shift(k)) for k in (1, 3, 2)]
        gathered = lax.all_to_all(many, "row", 0, 0, tiled=True)
        side_shape = shape((zs, cells + 8, tile), F32)
        back, keep, give = call(
            product_kernel,
            (shape((rows, cells, tile), BACK), side_shape, side_shape),
            [SMEM, VMEM, HBM] + [VMEM] * 6,
            scratch=[
                pltpu.VMEM((panels, cells, tile), BF16),
                pltpu.VMEM((panels * slots, cells, tile), F32),
                pltpu.VMEM((panels, cells, tile), F32),
                pltpu.VMEM((panels - KEPT, FIRST, tile, tile), BF16),
                pltpu.VMEM((panels, slots - FIRST, tile, tile), BF16),
                pltpu.SemaphoreType.DMA((panels - KEPT,)),
                pltpu.SemaphoreType.DMA((panels,)),
            ],
            flops=2 * work,
            moved=tile_bytes,
        )(meta, near_tiles, stored, gathered, one, pair, *near)
        back = lax.all_to_all(back, "row", 0, 0, tiled=True)
        given = lax.ppermute(give, "col", swap)
        sums = keep + given
        sides = [sums[0]] + [lax.ppermute(sums[k], "col", shift(k)) for k in (1, 3, 2)]
        arrived = (back, *sides, scales)
        if step == 0:
            many, one, applied0, dots0, residual = call(
                first_kernel,
                (many_shape, one_shape, full, shape((8, 128), F32), full),
                [VMEM] * 6,
            )(*arrived)
        elif step + 1 < STEPS:
            many, one, residual = call(
                lambda *refs: middle_kernel(total_cells, *refs),
                (many_shape, one_shape, full),
                [VMEM] * 8,
            )(*arrived, applied0, dots0)
        else:
            norms, residual = call(
                lambda *refs: last_kernel(total_cells, *refs),
                (shape((rows * cols, 128), F32), full),
                [VMEM] * 8,
            )(*arrived, applied0, dots0)
    norms = lax.all_to_all(norms, ("row", "col"), 0, 0, tiled=True)
    embedding = call(
        lambda *refs: blend_kernel(total_cells, *refs), full, [VMEM] * 3
    )(norms, residual, start_basis)
    return (embedding, degrees.reshape(tile))


def solution(mesh):
    placed = (
        P("row", "col", None, None, None),
        P("row", "col", None),
        P("row", "col"),
        P(None, ("row", "col")),
    )
    return jax.shard_map(
        local,
        mesh=mesh,
        in_specs=placed,
        out_specs=(P(None, ("row", "col")), P(("row", "col"))),
        check_vma=False,
    )
```
